32 devices in a mesh: recon: 2 (over y), space: 4 (over z), grp: 4 (over x, core).
Axes of the slice: x: 2, y: 2, z: 4, core: 2. Of those that a mesh axis runs over, the one named last changes fastest.
Arguments:
- warm_sources: float32 [16, 16, 128, 256], P(('recon', 'grp'), 'space'), parts along dimension 0, may hold values from -16 to 16
- warm_detectors: float32 [16, 16, 128, 256], P(('recon', 'grp'), 'space'), parts along dimension 0, may hold values from -16 to 16
- source_positions: int32 [16], P(('recon', 'grp')), parts along dimension 0, may hold values from 0 to 4095
- detector_positions: int32 [16], P(('recon', 'grp')), parts along dimension 0, may hold values from 0 to 4095
- labels: int32 [32, 128, 256], P(('recon', 'space')), parts along dimension 0, may hold values from 0 to 7
- absorption: float32 [8], replicated, may hold values from 0.02 to 0.6
- residual_codes: int32 [16, 8], P('recon'), parts along dimension 0, may hold values from -64 to 63
Outputs:
- source_fields: float32 [16, 16, 128, 256], P(('recon', 'grp'), 'space'), parts along dimension 0
- detector_fields: float32 [16, 16, 128, 256], P(('recon', 'grp'), 'space'), parts along dimension 0
- gradient: float32 [32, 128, 256], P(('recon', 'space'), 'grp'), parts along dimension 0
The draws below stay inside these ranges and needn't reach their ends.
There are 2 independent parts, one for each index of `recon`. The reference program is written for one: setup_inputs(seed, part) draws one part's arguments, and reference() takes and returns one part's arrays. A program takes and returns all parts, laid end to end along the dimension named above; an argument that names none is the same for every part. Nothing has to cross between parts.
All inputs are finite; a program needn't handle non-finite values.
Results may differ from the reference program's by a relative error of at most 0.0055.
Values may be sent and summed in bfloat16 or wider, within the bound.
A program may use at most 64 MiB of HBM per device.

```python
import math
import jax
import jax.numpy as jnp
from jax import lax

LX = 128
LY = 256
ITERS = 2
REGIONS = 8
NZ = 16
SOURCES = 8
DETECTORS = 8


def ramp_field(key, count):
    depth = (jnp.arange(NZ, dtype=jnp.float32) / jnp.float32(NZ - 1))[None, :, None, None]
    noise = jnp.clip(jax.random.normal(key, (count, NZ, LX, LY), jnp.float32), -4.0, 4.0)
    level = 0.3 * jnp.power(jnp.float32(10.0), depth)
    return level * (1.0 - depth + depth * noise)


def draw_warm_sources(key, part):
    return ramp_field(jax.random.fold_in(key, 11), SOURCES)


def draw_warm_detectors(key, part):
    return ramp_field(jax.random.fold_in(key, 23), DETECTORS)


def place_ends(array, key, least, largest):
    spot = [jax.random.randint(jax.random.fold_in(key, axis), (), 0, length) for axis, length in enumerate(array.shape)]
    longest = array.shape.index(max(array.shape))
    next_to = spot[:longest] + [(spot[longest] + 1) % array.shape[longest]] + spot[longest + 1:]
    return array.at[tuple(spot)].set(least).at[tuple(next_to)].set(largest)


def setup_inputs(seed: int = 0, part: int = 0) -> dict:
    keys = jax.random.split(jax.random.key(seed), 8)
    own_keys = jax.random.split(jax.random.fold_in(keys[7], part), 8)
    return {
        "warm_sources": draw_warm_sources(jax.random.fold_in(jax.random.fold_in(keys[7], part), 71), part),
        "warm_detectors": draw_warm_detectors(jax.random.fold_in(jax.random.fold_in(keys[7], part), 71), part),
        "source_positions": place_ends(jax.random.randint(own_keys[2], (SOURCES,), 0, NZ * LY), jax.random.fold_in(own_keys[2], 1), 0, (NZ * LY) - 1).astype(jnp.int32),
        "detector_positions": place_ends(jax.random.randint(own_keys[3], (DETECTORS,), 0, NZ * LY), jax.random.fold_in(own_keys[3], 1), 0, (NZ * LY) - 1).astype(jnp.int32),
        "labels": place_ends(jax.random.randint(own_keys[4], (NZ, LX, LY), 0, REGIONS), jax.random.fold_in(own_keys[4], 1), 0, REGIONS - 1).astype(jnp.int32),
        "absorption": jnp.clip(jnp.exp(jax.random.uniform(keys[5], (REGIONS,), jnp.float32, math.log(0.02), math.log(0.6))), 0.02, 0.6),
        "residual_codes": place_ends(jax.random.randint(own_keys[6], (SOURCES, DETECTORS), -64, 64), jax.random.fold_in(own_keys[6], 1), -64, 63).astype(jnp.int32),
    }


source_power = 50.0
code_scale = 1.0 / 1024.0


def operate(field, diagonal):
    padded = jnp.pad(field, 1)
    beside = padded[2:, 1:-1, 1:-1] + padded[:-2, 1:-1, 1:-1]
    beside = beside + padded[1:-1, 2:, 1:-1] + padded[1:-1, :-2, 1:-1]
    beside = beside + padded[1:-1, 1:-1, 2:] + padded[1:-1, 1:-1, :-2]
    return diagonal * field - beside


def point_drive(position, x_face):
    plane_at = position // LY
    column_at = position % LY
    plane_ids = jnp.arange(NZ, dtype=jnp.int32)[:, None, None]
    row_ids = jnp.arange(LX, dtype=jnp.int32)[None, :, None]
    column_ids = jnp.arange(LY, dtype=jnp.int32)[None, None, :]
    hit = (plane_ids == plane_at) & (row_ids == x_face) & (column_ids == column_at)
    return jnp.where(hit, jnp.float32(source_power), jnp.float32(0.0))


def solve(drive, start, diagonal):
    field = start
    residual = drive - operate(field, diagonal)
    direction = residual
    norm_now = jnp.sum(residual * residual)
    for sweep in range(ITERS):
        image = operate(direction, diagonal)
        alpha = norm_now / jnp.sum(direction * image)
        field = field + alpha * direction
        residual = residual - alpha * image
        if sweep + 1 < ITERS:
            norm_next = jnp.sum(residual * residual)
            direction = residual + (norm_next / norm_now) * direction
            norm_now = norm_next
    return field


def reference(warm_sources, warm_detectors, source_positions, detector_positions, labels, absorption, residual_codes):
    diagonal = 6.0 + absorption[labels]

    def one_source(item):
        return solve(point_drive(item[1], 0), item[0], diagonal)

    def one_detector(item):
        return solve(point_drive(item[1], LX - 1), item[0], diagonal)

    source_fields = lax.map(one_source, (warm_sources, source_positions))
    detector_fields = lax.map(one_detector, (warm_detectors, detector_positions))
    weights = (residual_codes.astype(jnp.float32) * code_scale).astype(jnp.bfloat16)
    rounded_detectors = detector_fields.astype(jnp.bfloat16).reshape(DETECTORS, -1)
    mixed = jnp.dot(weights, rounded_detectors, preferred_element_type=jnp.float32)
    rounded_sources = lax.optimization_barrier(source_fields.astype(jnp.bfloat16)).astype(jnp.float32)
    gradient = -jnp.sum(rounded_sources.reshape(SOURCES, -1) * mixed, axis=0)
    return source_fields, detector_fields, gradient.reshape(NZ, LX, LY)
```

```python
import functools

import jax
import jax.numpy as jnp
from jax import lax
from jax.experimental import pallas as pl
from jax.experimental.pallas import tpu as pltpu
from jax.sharding import PartitionSpec as P

source_power = 50.0
code_scale = 1.0 / 1024.0
PAD = 8
ROWS = 32
MESH = pl.DeviceIdType.MESH


def each(count, body):
    if count <= 8:
        for i in range(count):
            body(i)
    else:
        lax.fori_loop(0, count, lambda i, c: (body(i), c)[1], 0)


def kernel(
    n_space, n_grp,
    src_pos, det_pos, absorption, codes, warm_sources, warm_detectors, labels,
    out_sources, out_detectors, out_gradient,
    x, v0, v1, diag, lab, halo_send, halo_recv, half_send, half_recv,
    parts, packed, gathered, mixed,
    load_sem, store_sem, halo_ssem, halo_rsem, part_ssem, part_rsem, a2a_ssem, a2a_rsem,
):
    f32, bf16 = jnp.float32, jnp.bfloat16
    n_src, planes, breadth, extent = warm_sources.shape
    n_det = warm_detectors.shape[0]
    n_fields = n_src + n_det
    half = breadth // 2
    owned = breadth // n_grp
    k = lax.axis_index("space")
    g = lax.axis_index("grp")
    has_down, has_up = k > 0, k < n_space - 1
    chunks = breadth // ROWS

    barrier = pltpu.get_barrier_semaphore()

    def greet_space(j):
        pl.semaphore_signal(barrier, inc=1, device_id={"space": lax.rem(k + 1 + j, n_space)}, device_id_type=MESH)

    def greet_grp(j):
        pl.semaphore_signal(barrier, inc=1, device_id={"grp": lax.rem(g + 1 + j, n_grp)}, device_id_type=MESH)

    each(n_space - 1, greet_space)
    each(n_grp - 1, greet_grp)

    def warm(f):
        return warm_detectors.at[f] if f < n_det else warm_sources.at[f - n_det]

    def out(f):
        return out_detectors.at[f] if f < n_det else out_sources.at[f - n_det]

    inner = pl.ds(PAD, breadth)
    loads = [
        pltpu.make_async_copy(warm(f), x.at[f, pl.ds(1, planes), inner], load_sem.at[f]) for f in range(n_fields)
    ]
    load_labels = pltpu.make_async_copy(labels, lab, load_sem.at[n_fields])
    loads[0].start()
    loads[1].start()
    load_labels.start()
    for f in range(2, n_fields):
        loads[f].start()

    border = jnp.zeros((PAD, extent), f32)
    for f in range(n_fields):
        for z in range(1, planes + 1):
            for buf in (x, v0, v1):
                buf[f, z, pl.ds(0, PAD)] = border
                buf[f, z, pl.ds(PAD + breadth, PAD)] = border

    def clear(side):
        halo_recv[:, :, side] = jnp.zeros((2, n_fields, breadth, extent), bf16)
        half_recv[:, side] = jnp.zeros((n_fields, half, extent), bf16)

    pl.when(jnp.logical_not(has_down))(lambda: clear(0))
    pl.when(jnp.logical_not(has_up))(lambda: clear(1))

    def halo_copy(stage, f, up):
        send, recv = (halo_send, halo_recv) if stage < 2 else (half_send, half_recv)
        at = (stage, f) if stage < 2 else (f,)
        return pltpu.make_async_remote_copy(
            src_ref=send.at[(*at, 1 if up else 0)],
            dst_ref=recv.at[(*at, 0 if up else 1)],
            send_sem=halo_ssem.at[stage, f, 1 if up else 0],
            recv_sem=halo_rsem.at[stage, f, 0 if up else 1],
            device_id={"space": k + 1 if up else k - 1},
            device_id_type=MESH,
        )

    def halo_start(stage, f):
        pl.when(has_up)(lambda: halo_copy(stage, f, True).start())
        pl.when(has_down)(lambda: halo_copy(stage, f, False).start())

    def halo_wait(stage, f):
        pl.when(has_down)(lambda: halo_copy(stage, f, True).wait_recv())
        pl.when(has_up)(lambda: halo_copy(stage, f, False).wait_recv())

    def halo_done(stage, f):
        pl.when(has_up)(lambda: halo_copy(stage, f, True).wait_send())
        pl.when(has_down)(lambda: halo_copy(stage, f, False).wait_send())

    def loop(body, carry):
        return lax.fori_loop(0, chunks, lambda i, c: body(pl.multiple_of(i * ROWS, ROWS), c), carry)

    col = lax.broadcasted_iota(jnp.int32, (ROWS, extent), 1)
    row = lax.broadcasted_iota(jnp.int32, (ROWS, extent), 0)
    first_col, last_col = col == 0, col == extent - 1

    def right(value):
        return jnp.where(first_col, 0.0, pltpu.roll(value, 1, 1))

    def left(value):
        return jnp.where(last_col, 0.0, pltpu.roll(value, extent - 1, 1))

    def window(buf, f, z, r):
        wide = buf[f, z, pl.ds(r, ROWS + 2 * PAD)]
        centre = wide[PAD:PAD + ROWS]
        after = wide[PAD + 1:PAD + ROWS + 1]
        before = wide[PAD - 1:PAD + ROWS - 1]
        return centre, before, after

    def applied(buf, f, z, r):
        centre, before, after = window(buf, f, z, r)
        beside = buf[f, z - 1, pl.ds(PAD + r, ROWS)] + buf[f, z + 1, pl.ds(PAD + r, ROWS)]
        beside = beside + before + after + right(centre) + left(centre)
        return centre, diag[z - 1, pl.ds(r, ROWS)] * centre - beside

    def fold(value):
        return jnp.sum(value.reshape(value.shape[0] // 8, 8, extent), axis=0)

    def unpack_halo(stage, buf, f):
        def body(r, c):
            buf[f, 0, pl.ds(PAD + r, ROWS)] = halo_recv[stage, f, 0, pl.ds(r, ROWS)].astype(f32)
            buf[f, planes + 1, pl.ds(PAD + r, ROWS)] = halo_recv[stage, f, 1, pl.ds(r, ROWS)].astype(f32)
            return c
        loop(body, 0)

    def make_diagonal():
        load_labels.wait()
        values = [absorption[i] for i in range(absorption.shape[0])]

        def body(r, c):
            for z in range(planes):
                label = lab[z, pl.ds(r, ROWS)]
                value = jnp.full((ROWS, extent), values[0], f32)
                for region in range(1, len(values)):
                    value = jnp.where(label == region, values[region], value)
                diag[z, pl.ds(r, ROWS)] = 6.0 + value
            return c
        loop(body, 0)

    zero = jnp.zeros((8, extent), f32)
    sums = [None] * n_fields

    def pack_start(f):
        loads[f].wait()

        def body(r, c):
            halo_send[0, f, 0, pl.ds(r, ROWS)] = x[f, 1, pl.ds(PAD + r, ROWS)].astype(bf16)
            halo_send[0, f, 1, pl.ds(r, ROWS)] = x[f, planes, pl.ds(PAD + r, ROWS)].astype(bf16)
            return c
        loop(body, 0)

    def stage0(f):
        pack_start(f)
        halo_start(0, f)

    ends, middle = (1, planes), tuple(range(2, planes))
    face = [breadth - 1] * n_det + [0] * n_src

    def residual(f, zs, send, acc):
        position = det_pos[f] if f < n_det else src_pos[f - n_det]

        def body(r, acc):
            on_face = row + r == face[f]
            for z in zs:
                code = (k * planes + (z - 1)) * extent + col
                drive = jnp.where(on_face & (code == position), source_power, 0.0)
                value = drive - applied(x, f, z, r)[1]
                v0[f, z, pl.ds(PAD + r, ROWS)] = value
                if send and z == 1:
                    halo_send[1, f, 0, pl.ds(r, ROWS)] = value.astype(bf16)
                if send and z == planes:
                    halo_send[1, f, 1, pl.ds(r, ROWS)] = value.astype(bf16)
                acc = acc + fold(value * value)
            return acc
        return loop(body, acc)

    def stage1(f):
        acc = residual(f, middle, False, zero)
        halo_wait(0, f)
        unpack_halo(0, x, f)
        acc = residual(f, ends, True, acc)
        halo_start(1, f)
        sums[f] = (acc,)

    def second(f, zs, acc):
        def body(r, acc):
            m01, m11 = acc
            for z in zs:
                centre, value = applied(v0, f, z, r)
                v1[f, z, pl.ds(PAD + r, ROWS)] = value
                m01 = m01 + fold(centre * value)
                m11 = m11 + fold(value * value)
            return m01, m11
        return loop(body, acc)

    def stage2(f):
        acc = second(f, middle, (zero, zero))
        halo_wait(1, f)
        unpack_halo(1, v0, f)
        acc = second(f, ends, acc)
        half_send[f, 0] = v1[f, 1, pl.ds(PAD + half, half)].astype(bf16)
        half_send[f, 1] = v1[f, planes, pl.ds(PAD, half)].astype(bf16)
        halo_start(2, f)

        def body(r, m12):
            for z in range(1, planes + 1):
                centre, _, after = window(v1, f, z, r)
                beside = after + right(centre)
                if z < planes:
                    beside = beside + v1[f, z + 1, pl.ds(PAD + r, ROWS)]
                m12 = m12 + fold(centre * (diag[z - 1, pl.ds(r, ROWS)] * centre - 2.0 * beside))
            return m12
        sums[f] = (*sums[f], *acc, loop(body, zero))

    def part_copy(f, mine, peer):
        return pltpu.make_async_remote_copy(
            src_ref=parts.at[f, mine],
            dst_ref=parts.at[f, mine],
            send_sem=part_ssem.at[f, peer],
            recv_sem=part_rsem.at[f, mine],
            device_id={"space": peer},
            device_id_type=MESH,
        )

    def stage3(f):
        halo_wait(2, f)
        m00, m01, m11, m12 = sums[f]
        below = half_recv[f, 0].astype(f32) * v1[f, 1, pl.ds(PAD, half)]
        above = half_recv[f, 1].astype(f32) * v1[f, planes, pl.ds(PAD + half, half)]
        m12 = m12 - 2.0 * fold(below + above)
        which = lax.broadcasted_iota(jnp.int32, (8, 128), 0)
        tile = jnp.zeros((8, 128), f32)
        for j, m in enumerate((m00, m01, m11, m12)):
            m = jnp.sum(m, axis=0, keepdims=True)
            total = m[:, :128]
            for lane in range(128, extent, 128):
                total = total + m[:, lane:lane + 128]
            tile = jnp.where(which == j, total, tile)
        parts[f, k] = tile
        each(n_space - 1, lambda j: part_copy(f, k, lax.rem(k + 1 + j, n_space)).start())

    def a2a_copy(f, owner, peer):
        return pltpu.make_async_remote_copy(
            src_ref=packed.at[f, :, pl.ds(pl.multiple_of(peer * owned, owned), owned)],
            dst_ref=gathered.at[f, owner],
            send_sem=a2a_ssem.at[f, peer],
            recv_sem=a2a_rsem.at[f, owner],
            device_id={"grp": peer},
            device_id_type=MESH,
        )

    def stage4(f):
        each(n_space - 1, lambda j: part_copy(f, lax.rem(k + 1 + j, n_space), k).wait_recv())
        if n_space <= 8:
            total = parts[f, 0]
            for j in range(1, n_space):
                total = total + parts[f, j]
        else:
            total = lax.fori_loop(0, n_space, lambda j, t: t + parts[f, j], jnp.zeros((8, 128), f32))
        total = jnp.sum(total, axis=1, keepdims=True)
        m00, m01, m11, m12 = (total[j:j + 1] for j in range(4))
        alpha0 = m00 / m01
        norm1 = jnp.maximum(alpha0 * alpha0 * m11 - m00, 0.0)
        more = 1.0 + norm1 / m00
        curve = more * more * m01 - 2.0 * more * alpha0 * m11 + alpha0 * alpha0 * m12
        alpha1 = jnp.minimum(jnp.maximum(norm1 / curve, 1.0 / 12.7), 1.0 / 0.0199)
        c0 = alpha0 + alpha1 * more
        c1 = -alpha1 * alpha0

        def body(r, c):
            for z in range(1, planes + 1):
                rows = pl.ds(PAD + r, ROWS)
                value = x[f, z, rows] + c0 * v0[f, z, rows] + c1 * v1[f, z, rows]
                x[f, z, rows] = value
                packed[f, z - 1, pl.ds(r, ROWS)] = value.astype(bf16)
            return c
        loop(body, 0)
        each(n_grp - 1, lambda j: a2a_copy(f, g, lax.rem(g + 1 + j, n_grp)).start())
        pltpu.make_async_copy(x.at[f, pl.ds(1, planes), inner], out(f), store_sem.at[f]).start()
        gathered[f, g] = packed[f, :, pl.ds(pl.multiple_of(g * owned, owned), owned)]

    def stage5(f):
        each(n_grp - 1, lambda j: a2a_copy(f, lax.rem(g + 1 + j, n_grp), g).wait_recv())
        if f < n_det - 1:
            return
        step = 16
        if f == n_det - 1:
            def body(i, c):
                r = pl.multiple_of(i * step, step)
                for z in range(planes):
                    held = [
                        gathered[d % n_det, d // n_det, z, pl.ds(r, step)].astype(f32) for d in range(n_grp * n_det)
                    ]
                    for s in range(n_grp * n_src):
                        total = held[0] * (codes[s, 0].astype(f32) * code_scale)
                        for d in range(1, n_grp * n_det):
                            total = total + held[d] * (codes[s, d].astype(f32) * code_scale)
                        mixed[s, z, pl.ds(r, step)] = total
                return c
            lax.fori_loop(0, owned // step, body, 0)
            return

        def body(i, c):
            r = pl.multiple_of(i * step, step)
            for z in range(planes):
                total = jnp.zeros((step, extent), f32)
                for q in range(n_grp):
                    total = total - gathered[f, q, z, pl.ds(r, step)].astype(f32) * mixed[
                        q * n_src + f - n_det, z, pl.ds(r, step)
                    ]
                if f > n_det:
                    total = total + out_gradient[z, pl.ds(r, step)]
                out_gradient[z, pl.ds(r, step)] = total
            return c
        lax.fori_loop(0, owned // step, body, 0)

    pack_start(0)
    pack_start(1)
    pl.semaphore_wait(barrier, n_space - 1 + n_grp - 1)
    halo_start(0, 0)
    halo_start(0, 1)
    make_diagonal()

    stages = (stage0, stage1, stage2, stage3, stage4, stage5)
    for t in range(1, n_fields + 6):
        if 1 < t < n_fields:
            stage0(t)
        for s in range(5, 0, -1):
            if 0 <= t - s < n_fields:
                stages[s](t - s)

    for f in range(n_fields):
        for stage in range(3):
            halo_done(stage, f)
        each(n_space - 1, lambda j: part_copy(f, k, lax.rem(k + 1 + j, n_space)).wait_send())
        each(n_grp - 1, lambda j: a2a_copy(f, g, lax.rem(g + 1 + j, n_grp)).wait_send())
        pltpu.make_async_copy(x.at[f, pl.ds(1, planes), inner], out(f), store_sem.at[f]).wait()


def solution(mesh):
    n_space, n_grp = mesh.shape["space"], mesh.shape["grp"]

    def local(warm_sources, warm_detectors, source_positions, detector_positions, labels, absorption, residual_codes):
        n_src, planes, breadth, extent = warm_sources.shape
        n_det = warm_detectors.shape[0]
        n = n_src + n_det
        owned = breadth // n_grp
        f32, bf16 = jnp.float32, jnp.bfloat16
        smem = pl.BlockSpec(memory_space=pltpu.SMEM)
        hbm = pl.BlockSpec(memory_space=pl.ANY)
        vmem = pl.BlockSpec(memory_space=pltpu.VMEM)
        sem = pltpu.SemaphoreType.DMA
        tall = (n, planes + 2, breadth + 2 * PAD, extent)
        return pl.pallas_call(
            functools.partial(kernel, n_space, n_grp),
            out_shape=(
                jax.ShapeDtypeStruct(warm_sources.shape, f32),
                jax.ShapeDtypeStruct(warm_detectors.shape, f32),
                jax.ShapeDtypeStruct((planes, owned, extent), f32),
            ),
            in_specs=[smem] * 4 + [hbm] * 3,
            out_specs=(hbm, hbm, vmem),
            scratch_shapes=[
                pltpu.VMEM(tall, f32),
                pltpu.VMEM(tall, f32),
                pltpu.VMEM(tall, f32),
                pltpu.VMEM((planes, breadth, extent), f32),
                pltpu.VMEM((planes, breadth, extent), jnp.int32),
                pltpu.VMEM((2, n, 2, breadth, extent), bf16),
                pltpu.VMEM((2, n, 2, breadth, extent), bf16),
                pltpu.VMEM((n, 2, breadth // 2, extent), bf16),
                pltpu.VMEM((n, 2, breadth // 2, extent), bf16),
                pltpu.VMEM((n, n_space, 8, 128), f32),
                pltpu.VMEM((n, planes, breadth, extent), bf16),
                pltpu.VMEM((n, n_grp, planes, owned, extent), bf16),
                pltpu.VMEM((n_grp * n_src, planes, owned, extent), f32),
                sem((n + 1,)),
                sem((n,)),
                sem((3, n, 2)),
                sem((3, n, 2)),
                sem((n, n_space)),
                sem((n, n_space)),
                sem((n, n_grp)),
                sem((n, n_grp)),
            ],
            compiler_params=pltpu.CompilerParams(
                collective_id=0, has_side_effects=True, vmem_limit_bytes=40 * 1024 * 1024
            ),
        )(source_positions, detector_positions, absorption, residual_codes, warm_sources, warm_detectors, labels)

    fields = P(("recon", "grp"), "space", None, None)
    return jax.shard_map(
        local,
        mesh=mesh,
        in_specs=(
            fields,
            fields,
            P(("recon", "grp")),
            P(("recon", "grp")),
            P(("recon", "space"), None, None),
            P(),
            P("recon", None),
        ),
        out_specs=(fields, fields, P(("recon", "space"), "grp", None)),
        check_vma=False,
    )
```

```python
import functools

import jax
import jax.numpy as jnp
from jax import lax
from jax.experimental import pallas as pl
from jax.experimental.pallas import tpu as pltpu
from jax.sharding import PartitionSpec as P

source_power = 50.0
code_scale = 1.0 / 1024.0
PAD = 8
ROWS = 32
HALO = 3
MESH = pl.DeviceIdType.MESH


def each(count, body):
    if count <= 8:
        for i in range(count):
            body(i)
    else:
        lax.fori_loop(0, count, lambda i, c: (body(i), c)[1], 0)


def kernel(
    n_space, n_grp,
    src_pos_hbm, det_pos_hbm, absorption_hbm, codes_hbm, warm_sources, warm_detectors, labels,
    out_sources, out_detectors, out_gradient,
    x, v0, v1, diag, lab, halo_send, halo_recv, lab_send, lab_recv,
    parts, packed, gathered, mixed,
    src_pos, det_pos, absorption, codes, scalar_sem,
    load_sem, store_sem, halo_ssem, halo_rsem, part_ssem, part_rsem, a2a_ssem, a2a_rsem,
):
    f32, bf16 = jnp.float32, jnp.bfloat16
    n_src, planes, breadth, extent = warm_sources.shape
    n_det = warm_detectors.shape[0]
    n_fields = n_src + n_det
    half = breadth // 2
    owned = breadth // n_grp
    k = lax.axis_index("space")
    g = lax.axis_index("grp")
    has_down, has_up = k > 0, k < n_space - 1
    chunks = breadth // ROWS

    barrier = pltpu.get_barrier_semaphore()

    def greet_space(j):
        pl.semaphore_signal(barrier, inc=1, device_id={"space": lax.rem(k + 1 + j, n_space)}, device_id_type=MESH)

    def greet_grp(j):
        pl.semaphore_signal(barrier, inc=1, device_id={"grp": lax.rem(g + 1 + j, n_grp)}, device_id_type=MESH)

    each(n_space - 1, greet_space)
    each(n_grp - 1, greet_grp)

    def warm(f):
        return warm_detectors.at[f] if f < n_det else warm_sources.at[f - n_det]

    def out(f):
        return out_detectors.at[f] if f < n_det else out_sources.at[f - n_det]

    inner = pl.ds(PAD, breadth)
    loads = [
        pltpu.make_async_copy(warm(f), x.at[f, pl.ds(HALO, planes), inner], load_sem.at[f]) for f in range(n_fields)
    ]
    load_labels = pltpu.make_async_copy(labels, lab, load_sem.at[n_fields])
    scalars = [
        pltpu.make_async_copy(a, b, scalar_sem.at[i])
        for i, (a, b) in enumerate(
            ((absorption_hbm, absorption), (src_pos_hbm, src_pos), (det_pos_hbm, det_pos), (codes_hbm, codes))
        )
    ]
    loads[0].start()
    loads[1].start()
    load_labels.start()
    for copy in scalars:
        copy.start()
    for f in range(2, n_fields):
        loads[f].start()

    border = jnp.zeros((PAD, extent), f32)
    for f in range(n_fields):
        for z in range(HALO - 2, HALO + planes + 2):
            for buf in (x, v0, v1):
                buf[f, z, pl.ds(0, PAD)] = border
                buf[f, z, pl.ds(PAD + breadth, PAD)] = border

    def clear(side):
        halo_recv[:, side] = jnp.zeros(halo_recv.shape[:1] + halo_recv.shape[2:], bf16)
        lab_recv[side] = jnp.zeros(lab_recv.shape[1:], bf16)

    pl.when(jnp.logical_not(has_down))(lambda: clear(0))
    pl.when(jnp.logical_not(has_up))(lambda: clear(1))
    inside = (jnp.where(has_down, 1.0, 0.0), jnp.where(has_up, 1.0, 0.0))

    def halo_copy(f, up):
        send, recv = (halo_send.at[f], halo_recv.at[f]) if f < n_fields else (lab_send, lab_recv)
        return pltpu.make_async_remote_copy(
            src_ref=send.at[1 if up else 0],
            dst_ref=recv.at[0 if up else 1],
            send_sem=halo_ssem.at[f, 1 if up else 0],
            recv_sem=halo_rsem.at[f, 0 if up else 1],
            device_id={"space": k + 1 if up else k - 1},
            device_id_type=MESH,
        )

    def halo_start(f):
        pl.when(has_up)(lambda: halo_copy(f, True).start())
        pl.when(has_down)(lambda: halo_copy(f, False).start())

    def halo_wait(f):
        pl.when(has_down)(lambda: halo_copy(f, True).wait_recv())
        pl.when(has_up)(lambda: halo_copy(f, False).wait_recv())

    def halo_done(f):
        pl.when(has_up)(lambda: halo_copy(f, True).wait_send())
        pl.when(has_down)(lambda: halo_copy(f, False).wait_send())

    def loop(body, carry):
        return lax.fori_loop(0, chunks, lambda i, c: body(pl.multiple_of(i * ROWS, ROWS), c), carry)

    def half_loop(body, carry):
        return lax.fori_loop(0, chunks // 2, lambda i, c: body(pl.multiple_of(i * ROWS, ROWS), c), carry)

    col = lax.broadcasted_iota(jnp.int32, (ROWS, extent), 1)
    row = lax.broadcasted_iota(jnp.int32, (ROWS, extent), 0)
    first_col, last_col = col == 0, col == extent - 1

    def right(value):
        return jnp.where(first_col, 0.0, pltpu.roll(value, 1, 1))

    def left(value):
        return jnp.where(last_col, 0.0, pltpu.roll(value, extent - 1, 1))

    def window(buf, f, z, r):
        wide = buf[f, z + HALO, pl.ds(r, ROWS + 2 * PAD)]
        centre = wide[PAD:PAD + ROWS]
        after = wide[PAD + 1:PAD + ROWS + 1]
        before = wide[PAD - 1:PAD + ROWS - 1]
        return centre, before, after

    def applied(buf, f, z, r):
        centre, before, after = window(buf, f, z, r)
        rows = pl.ds(PAD + r, ROWS)
        beside = buf[f, z + HALO - 1, rows] + buf[f, z + HALO + 1, rows]
        beside = beside + before + after + right(centre) + left(centre)
        return centre, diag[z + 2, pl.ds(r, ROWS)] * centre - beside

    def fold(value):
        return jnp.sum(value.reshape(value.shape[0] // 8, 8, extent), axis=0)

    def make_diagonal():
        for copy in scalars:
            copy.wait()
        values = [absorption[i] for i in range(absorption.shape[0])]

        def body(r, c):
            for z in range(planes):
                diag[z + 2, pl.ds(r, ROWS)] = 6.0 + looked_up(lab[z, pl.ds(r, ROWS)], values)
            return c
        loop(body, 0)
        return values

    def looked_up(label, values):
        value = jnp.full((ROWS, extent), values[0], f32)
        for region in range(1, len(values)):
            value = jnp.where(label == region, values[region], value)
        return value

    def outer_diagonal(values):
        halo_wait(n_fields)

        def body(r, c):
            for side, z in ((0, -1), (1, planes)):
                label = lab_recv[side, pl.ds(r, ROWS)].astype(f32)
                diag[z + 2, pl.ds(r, ROWS)] = 6.0 + looked_up(label, values)
            return c
        loop(body, 0)

        def half_body(r, c):
            for side, z in ((0, -2), (1, planes + 1)):
                label = lab_recv[side, pl.ds(breadth + r, ROWS)].astype(f32)
                diag[z + 2, pl.ds(side * half + r, ROWS)] = 6.0 + looked_up(label, values)
            return c
        half_loop(half_body, 0)

    def labels_start():
        load_labels.wait()

        def body(r, c):
            rows = pl.ds(r, ROWS)
            lab_send[0, rows] = lab[0, rows].astype(f32).astype(bf16)
            lab_send[1, rows] = lab[planes - 1, rows].astype(f32).astype(bf16)
            return c
        loop(body, 0)

        def half_body(r, c):
            to = pl.ds(breadth + r, ROWS)
            lab_send[0, to] = lab[1, pl.ds(half + r, ROWS)].astype(f32).astype(bf16)
            lab_send[1, to] = lab[planes - 2, pl.ds(r, ROWS)].astype(f32).astype(bf16)
            return c
        half_loop(half_body, 0)
        halo_start(n_fields)

    zero = jnp.zeros((8, extent), f32)
    sums = [None] * n_fields

    def pack(f):
        loads[f].wait()

        def body(r, c):
            rows = pl.ds(PAD + r, ROWS)
            for depth in range(2):
                to = pl.ds(depth * breadth + r, ROWS)
                halo_send[f, 0, to] = x[f, HALO + depth, rows].astype(bf16)
                halo_send[f, 1, to] = x[f, HALO + planes - 1 - depth, rows].astype(bf16)
            return c
        loop(body, 0)

        def half_body(r, c):
            to = pl.ds(2 * breadth + r, ROWS)
            halo_send[f, 0, to] = x[f, HALO + 2, pl.ds(PAD + half + r, ROWS)].astype(bf16)
            halo_send[f, 1, to] = x[f, HALO + planes - 3, pl.ds(PAD + r, ROWS)].astype(bf16)
            return c
        half_loop(half_body, 0)

    def unpack(f):
        def body(r, c):
            rows = pl.ds(PAD + r, ROWS)
            for depth in range(2):
                at = pl.ds(depth * breadth + r, ROWS)
                x[f, HALO - 1 - depth, rows] = halo_recv[f, 0, at].astype(f32)
                x[f, HALO + planes + depth, rows] = halo_recv[f, 1, at].astype(f32)
            return c
        loop(body, 0)

        def half_body(r, c):
            at = pl.ds(2 * breadth + r, ROWS)
            x[f, HALO - 3, pl.ds(PAD + r, ROWS)] = halo_recv[f, 0, at].astype(f32)
            x[f, HALO + planes + 2, pl.ds(PAD + half + r, ROWS)] = halo_recv[f, 1, at].astype(f32)
            return c
        half_loop(half_body, 0)

    face = [breadth - 1] * n_det + [0] * n_src

    def residual(f, z, r):
        position = det_pos[f] if f < n_det else src_pos[f - n_det]
        code = (k * planes + z) * extent + col
        drive = jnp.where((row + r == face[f]) & (code == position), source_power, 0.0)
        value = drive - applied(x, f, z, r)[1]
        if z < 0:
            value = value * inside[0]
        elif z >= planes:
            value = value * inside[1]
        v0[f, z + HALO, pl.ds(PAD + r, ROWS)] = value
        return value

    def stage1(f):
        def body(r, acc):
            for z in range(1, planes - 1):
                value = residual(f, z, r)
                acc = acc + fold(value * value)
            return acc
        sums[f] = loop(body, zero)

    def stage2(f):
        halo_wait(f)
        unpack(f)

        def outer(r, acc):
            for z in (0, planes - 1):
                value = residual(f, z, r)
                acc = acc + fold(value * value)
            for z in (-1, planes):
                residual(f, z, r)
            return acc
        m00 = loop(outer, sums[f])

        def outer_half(r, c):
            residual(f, -2, r)
            residual(f, planes + 1, half + r)
            return c
        half_loop(outer_half, 0)

        def image(r, acc):
            m01, m11 = acc
            for z in range(planes):
                centre, value = applied(v0, f, z, r)
                v1[f, z + HALO, pl.ds(PAD + r, ROWS)] = value
                m01 = m01 + fold(centre * value)
                m11 = m11 + fold(value * value)
            return m01, m11
        m01, m11 = loop(image, (zero, zero))

        def curvature(r, m12):
            for z in range(planes):
                centre, _, after = window(v1, f, z, r)
                beside = after + right(centre)
                if z < planes - 1:
                    beside = beside + v1[f, z + HALO + 1, pl.ds(PAD + r, ROWS)]
                m12 = m12 + fold(centre * (diag[z + 2, pl.ds(r, ROWS)] * centre - 2.0 * beside))
            return m12
        m12 = loop(curvature, zero)

        def across(r, m12):
            below = applied(v0, f, -1, r)[1] * v1[f, HALO, pl.ds(PAD + r, ROWS)]
            above = applied(v0, f, planes, half + r)[1] * v1[f, HALO + planes - 1, pl.ds(PAD + half + r, ROWS)]
            return m12 - 2.0 * fold(inside[0] * below + inside[1] * above)
        m12 = half_loop(across, m12)
        send_sums(f, m00, m01, m11, m12)

    def part_copy(f, mine, peer):
        return pltpu.make_async_remote_copy(
            src_ref=parts.at[f, mine],
            dst_ref=parts.at[f, mine],
            send_sem=part_ssem.at[f, peer],
            recv_sem=part_rsem.at[f, mine],
            device_id={"space": peer},
            device_id_type=MESH,
        )

    def send_sums(f, m00, m01, m11, m12):
        which = lax.broadcasted_iota(jnp.int32, (8, 128), 0)
        tile = jnp.zeros((8, 128), f32)
        for j, m in enumerate((m00, m01, m11, m12)):
            m = jnp.sum(m, axis=0, keepdims=True)
            total = m[:, :128]
            for lane in range(128, extent, 128):
                total = total + m[:, lane:lane + 128]
            tile = jnp.where(which == j, total, tile)
        parts[f, k] = tile
        each(n_space - 1, lambda j: part_copy(f, k, lax.rem(k + 1 + j, n_space)).start())

    def a2a_copy(f, owner, peer):
        return pltpu.make_async_remote_copy(
            src_ref=packed.at[f, :, pl.ds(pl.multiple_of(peer * owned, owned), owned)],
            dst_ref=gathered.at[f, owner],
            send_sem=a2a_ssem.at[f, peer],
            recv_sem=a2a_rsem.at[f, owner],
            device_id={"grp": peer},
            device_id_type=MESH,
        )

    def stage4(f):
        each(n_space - 1, lambda j: part_copy(f, lax.rem(k + 1 + j, n_space), k).wait_recv())
        if n_space <= 8:
            total = parts[f, 0]
            for j in range(1, n_space):
                total = total + parts[f, j]
        else:
            total = lax.fori_loop(0, n_space, lambda j, t: t + parts[f, j], jnp.zeros((8, 128), f32))
        total = jnp.sum(total, axis=1, keepdims=True)
        m00, m01, m11, m12 = (total[j:j + 1] for j in range(4))
        alpha0 = m00 / m01
        norm1 = jnp.maximum(alpha0 * alpha0 * m11 - m00, 0.0)
        more = 1.0 + norm1 / m00
        curve = more * more * m01 - 2.0 * more * alpha0 * m11 + alpha0 * alpha0 * m12
        alpha1 = jnp.minimum(jnp.maximum(norm1 / curve, 1.0 / 12.7), 1.0 / 0.0199)
        c0 = alpha0 + alpha1 * more
        c1 = -alpha1 * alpha0

        def body(r, c):
            rows = pl.ds(PAD + r, ROWS)
            for z in range(planes):
                at = (f, z + HALO, rows)
                value = x[at] + c0 * v0[at] + c1 * v1[at]
                x[at] = value
                packed[f, z, pl.ds(r, ROWS)] = value.astype(bf16)
            return c
        loop(body, 0)
        each(n_grp - 1, lambda j: a2a_copy(f, g, lax.rem(g + 1 + j, n_grp)).start())
        pltpu.make_async_copy(x.at[f, pl.ds(HALO, planes), inner], out(f), store_sem.at[f]).start()
        gathered[f, g] = packed[f, :, pl.ds(pl.multiple_of(g * owned, owned), owned)]

    def stage5(f):
        each(n_grp - 1, lambda j: a2a_copy(f, lax.rem(g + 1 + j, n_grp), g).wait_recv())
        if f < n_det - 1:
            return
        step = 16
        if f == n_det - 1:
            def body(i, c):
                r = pl.multiple_of(i * step, step)
                for z in range(planes):
                    held = [
                        gathered[d % n_det, d // n_det, z, pl.ds(r, step)].astype(f32) for d in range(n_grp * n_det)
                    ]
                    for s in range(n_grp * n_src):
                        total = held[0] * (codes[s, 0].astype(f32) * code_scale)
                        for d in range(1, n_grp * n_det):
                            total = total + held[d] * (codes[s, d].astype(f32) * code_scale)
                        mixed[s, z, pl.ds(r, step)] = total
                return c
            lax.fori_loop(0, owned // step, body, 0)
            return

        def body(i, c):
            r = pl.multiple_of(i * step, step)
            for z in range(planes):
                total = jnp.zeros((step, extent), f32)
                for q in range(n_grp):
                    total = total - gathered[f, q, z, pl.ds(r, step)].astype(f32) * mixed[
                        q * n_src + f - n_det, z, pl.ds(r, step)
                    ]
                if f > n_det:
                    total = total + out_gradient[z, pl.ds(r, step)]
                out_gradient[z, pl.ds(r, step)] = total
            return c
        lax.fori_loop(0, owned // step, body, 0)

    pack(0)
    pl.semaphore_wait(barrier, n_space - 1 + n_grp - 1)
    halo_start(0)
    labels_start()
    for f in range(1, n_fields):
        pack(f)
        halo_start(f)
    values = make_diagonal()
    for f in range(n_fields):
        stage1(f)
    outer_diagonal(values)
    for t in range(n_fields + 3):
        if t < n_fields:
            stage2(t)
        if 0 <= t - 1 < n_fields:
            stage4(t - 1)
        if 0 <= t - 3 < n_fields:
            stage5(t - 3)

    halo_done(n_fields)
    for f in range(n_fields):
        halo_done(f)
        each(n_space - 1, lambda j: part_copy(f, k, lax.rem(k + 1 + j, n_space)).wait_send())
        each(n_grp - 1, lambda j: a2a_copy(f, g, lax.rem(g + 1 + j, n_grp)).wait_send())
        pltpu.make_async_copy(x.at[f, pl.ds(HALO, planes), inner], out(f), store_sem.at[f]).wait()


def hand_over(a, b, c, out_a, out_b, out_c, held_a, held_b, held_c, sems):
    triples = ((a, held_a, out_a), (b, held_b, out_b), (c, held_c, out_c))
    inward = [pltpu.make_async_copy(i, h, sems.at[0, j]) for j, (i, h, _) in enumerate(triples)]
    outward = [pltpu.make_async_copy(h, o, sems.at[1, j]) for j, (_, h, o) in enumerate(triples)]
    for copy in inward:
        copy.start()
    for first, then in zip(inward, outward):
        first.wait()
        then.start()
    for copy in outward:
        copy.wait()


def solution(mesh):
    n_space, n_grp = mesh.shape["space"], mesh.shape["grp"]

    def local(warm_sources, warm_detectors, source_positions, detector_positions, labels, absorption, residual_codes):
        n_src, planes, breadth, extent = warm_sources.shape
        n_det = warm_detectors.shape[0]
        n = n_src + n_det
        owned = breadth // n_grp
        f32, bf16 = jnp.float32, jnp.bfloat16
        hbm = pl.BlockSpec(memory_space=pl.ANY)
        vmem = pl.BlockSpec(memory_space=pltpu.VMEM)
        sem = pltpu.SemaphoreType.DMA
        tall = (n, planes + 2 * HALO, breadth + 2 * PAD, extent)
        results = pl.pallas_call(
            functools.partial(kernel, n_space, n_grp),
            out_shape=(
                jax.ShapeDtypeStruct(warm_sources.shape, f32),
                jax.ShapeDtypeStruct(warm_detectors.shape, f32),
                jax.ShapeDtypeStruct((planes, owned, extent), f32),
            ),
            in_specs=[hbm] * 7,
            out_specs=(hbm, hbm, vmem),
            scratch_shapes=[
                pltpu.VMEM(tall, f32),
                pltpu.VMEM(tall, f32),
                pltpu.VMEM(tall, f32),
                pltpu.VMEM((planes + 4, breadth, extent), f32),
                pltpu.VMEM((planes, breadth, extent), jnp.int32),
                pltpu.VMEM((n, 2, 2 * breadth + breadth // 2, extent), bf16),
                pltpu.VMEM((n, 2, 2 * breadth + breadth // 2, extent), bf16),
                pltpu.VMEM((2, breadth + breadth // 2, extent), bf16),
                pltpu.VMEM((2, breadth + breadth // 2, extent), bf16),
                pltpu.VMEM((n, n_space, 8, 128), f32),
                pltpu.VMEM((n, planes, breadth, extent), bf16),
                pltpu.VMEM((n, n_grp, planes, owned, extent), bf16),
                pltpu.VMEM((n_grp * n_src, planes, owned, extent), f32),
                pltpu.SMEM(source_positions.shape, jnp.int32),
                pltpu.SMEM(detector_positions.shape, jnp.int32),
                pltpu.SMEM(absorption.shape, f32),
                pltpu.SMEM(residual_codes.shape, jnp.int32),
                sem((4,)),
                sem((n + 1,)),
                sem((n,)),
                sem((n + 1, 2)),
                sem((n + 1, 2)),
                sem((n, n_space)),
                sem((n, n_space)),
                sem((n, n_grp)),
                sem((n, n_grp)),
            ],
            compiler_params=pltpu.CompilerParams(
                collective_id=0, has_side_effects=True, vmem_limit_bytes=60 * 1024 * 1024
            ),
        )(source_positions, detector_positions, absorption, residual_codes, warm_sources, warm_detectors, labels)
        return pl.pallas_call(
            hand_over,
            out_shape=tuple(jax.ShapeDtypeStruct(r.shape, r.dtype) for r in results),
            in_specs=[hbm] * 3,
            out_specs=(hbm,) * 3,
            scratch_shapes=[*(pltpu.VMEM(r.shape, r.dtype) for r in results), sem((2, 3))],
        )(*results)

    fields = P(("recon", "grp"), "space", None, None)
    return jax.shard_map(
        local,
        mesh=mesh,
        in_specs=(
            fields,
            fields,
            P(("recon", "grp")),
            P(("recon", "grp")),
            P(("recon", "space"), None, None),
            P(),
            P("recon", None),
        ),
        out_specs=(fields, fields, P(("recon", "space"), "grp", None)),
        check_vma=False,
    )
```

```python
import functools

import jax
import jax.numpy as jnp
from jax import lax
from jax.experimental import pallas as pl
from jax.experimental.pallas import tpu as pltpu
from jax.sharding import PartitionSpec as P

source_power = 50.0
code_scale = 1.0 / 1024.0
PAD = 8
ROWS = 32
HALO = 3
MESH = pl.DeviceIdType.MESH


def each(count, body):
    if count <= 8:
        for i in range(count):
            body(i)
    else:
        lax.fori_loop(0, count, lambda i, c: (body(i), c)[1], 0)


def kernel(
    n_space, n_grp,
    src_pos_hbm, det_pos_hbm, absorption_hbm, codes_hbm, warm_sources, warm_detectors, labels,
    out_sources, out_detectors, out_gradient,
    x, v0, v1, diag, lab, halo_send, halo_recv, lab_send, lab_recv,
    parts, packed, gathered, mixed,
    src_pos, det_pos, absorption, codes, scalar_sem,
    load_sem, store_sem, halo_ssem, halo_rsem, share_ssem, share_rsem, part_ssem, part_rsem, a2a_ssem, a2a_rsem,
):
    f32, bf16 = jnp.float32, jnp.bfloat16
    n_src, planes, breadth, extent = warm_sources.shape
    n_det = warm_detectors.shape[0]
    n_fields = n_src + n_det
    half = breadth // 2
    owned = breadth // n_grp
    k = lax.axis_index("space")
    g = lax.axis_index("grp")
    has_down, has_up = k > 0, k < n_space - 1
    chunks = breadth // ROWS

    barrier = pltpu.get_barrier_semaphore()

    def greet_space(j):
        pl.semaphore_signal(barrier, inc=1, device_id={"space": lax.rem(k + 1 + j, n_space)}, device_id_type=MESH)

    def greet_grp(j):
        pl.semaphore_signal(barrier, inc=1, device_id={"grp": lax.rem(g + 1 + j, n_grp)}, device_id_type=MESH)

    each(n_space - 1, greet_space)
    each(n_grp - 1, greet_grp)

    def warm(f):
        return warm_detectors.at[f] if f < n_det else warm_sources.at[f - n_det]

    def out(f):
        return out_detectors.at[f] if f < n_det else out_sources.at[f - n_det]

    inner = pl.ds(PAD, breadth)
    loads = [
        pltpu.make_async_copy(warm(f), x.at[f, pl.ds(HALO, planes), inner], load_sem.at[f]) for f in range(n_fields)
    ]
    load_labels = pltpu.make_async_copy(labels, lab, load_sem.at[n_fields])
    scalars = [
        pltpu.make_async_copy(a, b, scalar_sem.at[i])
        for i, (a, b) in enumerate(
            ((absorption_hbm, absorption), (src_pos_hbm, src_pos), (det_pos_hbm, det_pos), (codes_hbm, codes))
        )
    ]
    load_labels.start()
    loads[0].start()
    loads[1].start()
    for copy in scalars:
        copy.start()
    for f in range(2, n_fields):
        loads[f].start()

    def clear_borders():
        border = jnp.zeros((PAD, extent), f32)
        for f in range(n_fields):
            for z in range(HALO - 2, HALO + planes + 2):
                for buf in (x, v0, v1):
                    buf[f, z, pl.ds(0, PAD)] = border
                    buf[f, z, pl.ds(PAD + breadth, PAD)] = border

    def clear(side):
        halo_recv[:, side] = jnp.zeros(halo_recv.shape[:1] + halo_recv.shape[2:], bf16)
        lab_recv[side] = jnp.zeros(lab_recv.shape[1:], bf16)

    inside = (jnp.where(has_down, 1.0, 0.0), jnp.where(has_up, 1.0, 0.0))

    portion = lab_recv.shape[1] // n_grp

    def share(owner):
        return pl.ds(pl.multiple_of(owner * portion, 16), portion)

    def share_copy(side, owner, peer):
        return pltpu.make_async_remote_copy(
            src_ref=lab_recv.at[side, share(owner)],
            dst_ref=lab_recv.at[side, share(owner)],
            send_sem=share_ssem.at[side, peer],
            recv_sem=share_rsem.at[side, owner],
            device_id={"grp": peer},
            device_id_type=MESH,
        )

    def on_sides(body):
        pl.when(has_down)(lambda: body(0))
        pl.when(has_up)(lambda: body(1))

    def share_start(side):
        halo_copy(n_fields, side == 0).wait_recv()
        each(n_grp - 1, lambda j: share_copy(side, g, lax.rem(g + 1 + j, n_grp)).start())

    def share_wait(side):
        each(n_grp - 1, lambda j: share_copy(side, lax.rem(g + 1 + j, n_grp), g).wait_recv())

    def share_done(side):
        each(n_grp - 1, lambda j: share_copy(side, g, lax.rem(g + 1 + j, n_grp)).wait_send())

    def halo_copy(f, up):
        if f < n_fields:
            source, target = halo_send.at[f, 1 if up else 0], halo_recv.at[f, 0 if up else 1]
        else:
            source, target = lab_send.at[1 if up else 0, share(g)], lab_recv.at[0 if up else 1, share(g)]
        return pltpu.make_async_remote_copy(
            src_ref=source,
            dst_ref=target,
            send_sem=halo_ssem.at[f, 1 if up else 0],
            recv_sem=halo_rsem.at[f, 0 if up else 1],
            device_id={"space": k + 1 if up else k - 1},
            device_id_type=MESH,
        )

    def halo_start(f):
        pl.when(has_up)(lambda: halo_copy(f, True).start())
        pl.when(has_down)(lambda: halo_copy(f, False).start())

    def halo_wait(f):
        pl.when(has_down)(lambda: halo_copy(f, True).wait_recv())
        pl.when(has_up)(lambda: halo_copy(f, False).wait_recv())

    def halo_done(f):
        pl.when(has_up)(lambda: halo_copy(f, True).wait_send())
        pl.when(has_down)(lambda: halo_copy(f, False).wait_send())

    def loop(body, carry):
        return lax.fori_loop(0, chunks, lambda i, c: body(pl.multiple_of(i * ROWS, ROWS), c), carry)

    def half_loop(body, carry):
        return lax.fori_loop(0, chunks // 2, lambda i, c: body(pl.multiple_of(i * ROWS, ROWS), c), carry)

    col = lax.broadcasted_iota(jnp.int32, (ROWS, extent), 1)
    row = lax.broadcasted_iota(jnp.int32, (ROWS, extent), 0)
    first_col, last_col = col == 0, col == extent - 1

    def right(value):
        return jnp.where(first_col, 0.0, pltpu.roll(value, 1, 1))

    def left(value):
        return jnp.where(last_col, 0.0, pltpu.roll(value, extent - 1, 1))

    def window(buf, f, z, r):
        wide = buf[f, z + HALO, pl.ds(r, ROWS + 2 * PAD)]
        centre = wide[PAD:PAD + ROWS]
        after = wide[PAD + 1:PAD + ROWS + 1]
        before = wide[PAD - 1:PAD + ROWS - 1]
        return centre, before, after

    def applied(buf, f, z, r):
        centre, before, after = window(buf, f, z, r)
        rows = pl.ds(PAD + r, ROWS)
        beside = buf[f, z + HALO - 1, rows] + buf[f, z + HALO + 1, rows]
        beside = beside + before + after + right(centre) + left(centre)
        return centre, diag[z + 2, pl.ds(r, ROWS)] * centre - beside

    def fold(value):
        return jnp.sum(value.reshape(value.shape[0] // 8, 8, extent), axis=0)

    def make_diagonal():
        for copy in scalars:
            copy.wait()
        values = [absorption[i] for i in range(absorption.shape[0])]

        def body(r, c):
            for z in range(planes):
                diag[z + 2, pl.ds(r, ROWS)] = 6.0 + looked_up(lab[z, pl.ds(r, ROWS)], values)
            return c
        loop(body, 0)
        return values

    def looked_up(label, values):
        value = jnp.full((ROWS, extent), values[0], f32)
        for region in range(1, len(values)):
            value = jnp.where(label == region, values[region], value)
        return value

    def outer_diagonal(values):
        on_sides(share_wait)

        def body(r, c):
            for side, z in ((0, -1), (1, planes)):
                label = lab_recv[side, pl.ds(r, ROWS)].astype(f32)
                diag[z + 2, pl.ds(r, ROWS)] = 6.0 + looked_up(label, values)
            return c
        loop(body, 0)

        def half_body(r, c):
            for side, z in ((0, -2), (1, planes + 1)):
                label = lab_recv[side, pl.ds(breadth + r, ROWS)].astype(f32)
                diag[z + 2, pl.ds(side * half + r, ROWS)] = 6.0 + looked_up(label, values)
            return c
        half_loop(half_body, 0)

    def labels_pack():
        load_labels.wait()

        def body(r, c):
            rows = pl.ds(r, ROWS)
            lab_send[0, rows] = lab[0, rows].astype(f32).astype(bf16)
            lab_send[1, rows] = lab[planes - 1, rows].astype(f32).astype(bf16)
            return c
        loop(body, 0)

        def half_body(r, c):
            to = pl.ds(breadth + r, ROWS)
            lab_send[0, to] = lab[1, pl.ds(half + r, ROWS)].astype(f32).astype(bf16)
            lab_send[1, to] = lab[planes - 2, pl.ds(r, ROWS)].astype(f32).astype(bf16)
            return c
        half_loop(half_body, 0)

    zero = jnp.zeros((8, extent), f32)
    sums = [None] * n_fields

    def pack(f):
        loads[f].wait()

        def body(r, c):
            rows = pl.ds(PAD + r, ROWS)
            for depth in range(2):
                to = pl.ds(depth * breadth + r, ROWS)
                halo_send[f, 0, to] = x[f, HALO + depth, rows].astype(bf16)
                halo_send[f, 1, to] = x[f, HALO + planes - 1 - depth, rows].astype(bf16)
            return c
        loop(body, 0)

        def half_body(r, c):
            to = pl.ds(2 * breadth + r, ROWS)
            halo_send[f, 0, to] = x[f, HALO + 2, pl.ds(PAD + half + r, ROWS)].astype(bf16)
            halo_send[f, 1, to] = x[f, HALO + planes - 3, pl.ds(PAD + r, ROWS)].astype(bf16)
            return c
        half_loop(half_body, 0)

    def unpack(f):
        def body(r, c):
            rows = pl.ds(PAD + r, ROWS)
            for depth in range(2):
                at = pl.ds(depth * breadth + r, ROWS)
                x[f, HALO - 1 - depth, rows] = halo_recv[f, 0, at].astype(f32)
                x[f, HALO + planes + depth, rows] = halo_recv[f, 1, at].astype(f32)
            return c
        loop(body, 0)

        def half_body(r, c):
            at = pl.ds(2 * breadth + r, ROWS)
            x[f, HALO - 3, pl.ds(PAD + r, ROWS)] = halo_recv[f, 0, at].astype(f32)
            x[f, HALO + planes + 2, pl.ds(PAD + half + r, ROWS)] = halo_recv[f, 1, at].astype(f32)
            return c
        half_loop(half_body, 0)

    face = [breadth - 1] * n_det + [0] * n_src

    def residual(f, z, r):
        position = det_pos[f] if f < n_det else src_pos[f - n_det]
        code = (k * planes + z) * extent + col
        drive = jnp.where((row + r == face[f]) & (code == position), source_power, 0.0)
        value = drive - applied(x, f, z, r)[1]
        if z < 0:
            value = value * inside[0]
        elif z >= planes:
            value = value * inside[1]
        v0[f, z + HALO, pl.ds(PAD + r, ROWS)] = value
        return value

    def stage1(f):
        def body(r, acc):
            for z in range(1, planes - 1):
                value = residual(f, z, r)
                acc = acc + fold(value * value)
            return acc
        sums[f] = loop(body, zero)

    def stage2(f):
        halo_wait(f)
        unpack(f)

        def outer(r, acc):
            for z in (0, planes - 1):
                value = residual(f, z, r)
                acc = acc + fold(value * value)
            for z in (-1, planes):
                residual(f, z, r)
            return acc
        m00 = loop(outer, sums[f])

        def outer_half(r, c):
            residual(f, -2, r)
            residual(f, planes + 1, half + r)
            return c
        half_loop(outer_half, 0)

        def image(r, acc):
            m01, m11 = acc
            for z in range(planes):
                centre, value = applied(v0, f, z, r)
                v1[f, z + HALO, pl.ds(PAD + r, ROWS)] = value
                m01 = m01 + fold(centre * value)
                m11 = m11 + fold(value * value)
            return m01, m11
        m01, m11 = loop(image, (zero, zero))

        def curvature(r, m12):
            for z in range(planes):
                centre, _, after = window(v1, f, z, r)
                beside = after + right(centre)
                if z < planes - 1:
                    beside = beside + v1[f, z + HALO + 1, pl.ds(PAD + r, ROWS)]
                m12 = m12 + fold(centre * (diag[z + 2, pl.ds(r, ROWS)] * centre - 2.0 * beside))
            return m12
        m12 = loop(curvature, zero)

        def across(r, m12):
            below = applied(v0, f, -1, r)[1] * v1[f, HALO, pl.ds(PAD + r, ROWS)]
            above = applied(v0, f, planes, half + r)[1] * v1[f, HALO + planes - 1, pl.ds(PAD + half + r, ROWS)]
            return m12 - 2.0 * fold(inside[0] * below + inside[1] * above)
        m12 = half_loop(across, m12)
        send_sums(f, m00, m01, m11, m12)

    def part_copy(f, mine, peer):
        return pltpu.make_async_remote_copy(
            src_ref=parts.at[f, mine],
            dst_ref=parts.at[f, mine],
            send_sem=part_ssem.at[f, peer],
            recv_sem=part_rsem.at[f, mine],
            device_id={"space": peer},
            device_id_type=MESH,
        )

    def send_sums(f, m00, m01, m11, m12):
        which = lax.broadcasted_iota(jnp.int32, (8, 128), 0)
        tile = jnp.zeros((8, 128), f32)
        for j, m in enumerate((m00, m01, m11, m12)):
            m = jnp.sum(m, axis=0, keepdims=True)
            total = m[:, :128]
            for lane in range(128, extent, 128):
                total = total + m[:, lane:lane + 128]
            tile = jnp.where(which == j, total, tile)
        parts[f, k] = tile
        each(n_space - 1, lambda j: part_copy(f, k, lax.rem(k + 1 + j, n_space)).start())

    def a2a_copy(f, owner, peer):
        return pltpu.make_async_remote_copy(
            src_ref=packed.at[f, :, pl.ds(pl.multiple_of(peer * owned, owned), owned)],
            dst_ref=gathered.at[f, owner],
            send_sem=a2a_ssem.at[f, peer],
            recv_sem=a2a_rsem.at[f, owner],
            device_id={"grp": peer},
            device_id_type=MESH,
        )

    def stage4(f):
        each(n_space - 1, lambda j: part_copy(f, lax.rem(k + 1 + j, n_space), k).wait_recv())
        if n_space <= 8:
            total = parts[f, 0]
            for j in range(1, n_space):
                total = total + parts[f, j]
        else:
            total = lax.fori_loop(0, n_space, lambda j, t: t + parts[f, j], jnp.zeros((8, 128), f32))
        total = jnp.sum(total, axis=1, keepdims=True)
        m00, m01, m11, m12 = (total[j:j + 1] for j in range(4))
        alpha0 = m00 / m01
        norm1 = jnp.maximum(alpha0 * alpha0 * m11 - m00, 0.0)
        more = 1.0 + norm1 / m00
        curve = more * more * m01 - 2.0 * more * alpha0 * m11 + alpha0 * alpha0 * m12
        alpha1 = jnp.minimum(jnp.maximum(norm1 / curve, 1.0 / 12.7), 1.0 / 0.0199)
        c0 = alpha0 + alpha1 * more
        c1 = -alpha1 * alpha0

        def body(r, c):
            rows = pl.ds(PAD + r, ROWS)
            for z in range(planes):
                at = (f, z + HALO, rows)
                value = x[at] + c0 * v0[at] + c1 * v1[at]
                x[at] = value
                packed[f, z, pl.ds(r, ROWS)] = value.astype(bf16)
            return c
        loop(body, 0)
        each(n_grp - 1, lambda j: a2a_copy(f, g, lax.rem(g + 1 + j, n_grp)).start())
        pltpu.make_async_copy(x.at[f, pl.ds(HALO, planes), inner], out(f), store_sem.at[f]).start()
        gathered[f, g] = packed[f, :, pl.ds(pl.multiple_of(g * owned, owned), owned)]

    def stage5(f):
        each(n_grp - 1, lambda j: a2a_copy(f, lax.rem(g + 1 + j, n_grp), g).wait_recv())
        if f < n_det - 1:
            return
        step = 16
        if f == n_det - 1:
            def body(i, c):
                r = pl.multiple_of(i * step, step)
                for z in range(planes):
                    held = [
                        gathered[d % n_det, d // n_det, z, pl.ds(r, step)].astype(f32) for d in range(n_grp * n_det)
                    ]
                    for s in range(n_grp * n_src):
                        total = held[0] * (codes[s, 0].astype(f32) * code_scale)
                        for d in range(1, n_grp * n_det):
                            total = total + held[d] * (codes[s, d].astype(f32) * code_scale)
                        mixed[s, z, pl.ds(r, step)] = total
                return c
            lax.fori_loop(0, owned // step, body, 0)
            return

        def body(i, c):
            r = pl.multiple_of(i * step, step)
            for z in range(planes):
                total = jnp.zeros((step, extent), f32)
                for q in range(n_grp):
                    total = total - gathered[f, q, z, pl.ds(r, step)].astype(f32) * mixed[
                        q * n_src + f - n_det, z, pl.ds(r, step)
                    ]
                if f > n_det:
                    total = total + out_gradient[z, pl.ds(r, step)]
                out_gradient[z, pl.ds(r, step)] = total
            return c
        lax.fori_loop(0, owned // step, body, 0)

    labels_pack()
    pack(0)
    pl.semaphore_wait(barrier, n_space - 1 + n_grp - 1)
    halo_start(n_fields)
    halo_start(0)
    pack(1)
    halo_start(1)
    clear_borders()
    pl.when(jnp.logical_not(has_down))(lambda: clear(0))
    pl.when(jnp.logical_not(has_up))(lambda: clear(1))
    for f in range(2, n_fields):
        pack(f)
    values = make_diagonal()
    on_sides(share_start)
    for f in range(n_fields):
        stage1(f)
    outer_diagonal(values)
    for t in range(n_fields + 3):
        if t < n_fields:
            stage2(t)
            if t + 2 < n_fields:
                halo_start(t + 2)
        if 0 <= t - 1 < n_fields:
            stage4(t - 1)
        if 0 <= t - 3 < n_fields:
            stage5(t - 3)

    halo_done(n_fields)
    on_sides(share_done)
    for f in range(n_fields):
        halo_done(f)
        each(n_space - 1, lambda j: part_copy(f, k, lax.rem(k + 1 + j, n_space)).wait_send())
        each(n_grp - 1, lambda j: a2a_copy(f, g, lax.rem(g + 1 + j, n_grp)).wait_send())
        pltpu.make_async_copy(x.at[f, pl.ds(HALO, planes), inner], out(f), store_sem.at[f]).wait()


def hand_over(a, b, c, out_a, out_b, out_c, held_a, held_b, held_c, sems):
    triples = ((a, held_a, out_a), (b, held_b, out_b), (c, held_c, out_c))
    inward = [pltpu.make_async_copy(i, h, sems.at[0, j]) for j, (i, h, _) in enumerate(triples)]
    outward = [pltpu.make_async_copy(h, o, sems.at[1, j]) for j, (_, h, o) in enumerate(triples)]
    for copy in inward:
        copy.start()
    for first, then in zip(inward, outward):
        first.wait()
        then.start()
    for copy in outward:
        copy.wait()


def solution(mesh):
    n_space, n_grp = mesh.shape["space"], mesh.shape["grp"]

    def local(warm_sources, warm_detectors, source_positions, detector_positions, labels, absorption, residual_codes):
        n_src, planes, breadth, extent = warm_sources.shape
        n_det = warm_detectors.shape[0]
        n = n_src + n_det
        owned = breadth // n_grp
        f32, bf16 = jnp.float32, jnp.bfloat16
        hbm = pl.BlockSpec(memory_space=pl.ANY)
        vmem = pl.BlockSpec(memory_space=pltpu.VMEM)
        sem = pltpu.SemaphoreType.DMA
        tall = (n, planes + 2 * HALO, breadth + 2 * PAD, extent)
        results = pl.pallas_call(
            functools.partial(kernel, n_space, n_grp),
            out_shape=(
                jax.ShapeDtypeStruct(warm_sources.shape, f32),
                jax.ShapeDtypeStruct(warm_detectors.shape, f32),
                jax.ShapeDtypeStruct((planes, owned, extent), f32),
            ),
            in_specs=[hbm] * 7,
            out_specs=(hbm, hbm, vmem),
            scratch_shapes=[
                pltpu.VMEM(tall, f32),
                pltpu.VMEM(tall, f32),
                pltpu.VMEM(tall, f32),
                pltpu.VMEM((planes + 4, breadth, extent), f32),
                pltpu.VMEM((planes, breadth, extent), jnp.int32),
                pltpu.VMEM((n, 2, 2 * breadth + breadth // 2, extent), bf16),
                pltpu.VMEM((n, 2, 2 * breadth + breadth // 2, extent), bf16),
                pltpu.VMEM((2, breadth + breadth // 2, extent), bf16),
                pltpu.VMEM((2, breadth + breadth // 2, extent), bf16),
                pltpu.VMEM((n, n_space, 8, 128), f32),
                pltpu.VMEM((n, planes, breadth, extent), bf16),
                pltpu.VMEM((n, n_grp, planes, owned, extent), bf16),
                pltpu.VMEM((n_grp * n_src, planes, owned, extent), f32),
                pltpu.SMEM(source_positions.shape, jnp.int32),
                pltpu.SMEM(detector_positions.shape, jnp.int32),
                pltpu.SMEM(absorption.shape, f32),
                pltpu.SMEM(residual_codes.shape, jnp.int32),
                sem((4,)),
                sem((n + 1,)),
                sem((n,)),
                sem((n + 1, 2)),
                sem((n + 1, 2)),
                sem((2, n_grp)),
                sem((2, n_grp)),
                sem((n, n_space)),
                sem((n, n_space)),
                sem((n, n_grp)),
                sem((n, n_grp)),
            ],
            compiler_params=pltpu.CompilerParams(
                collective_id=0, has_side_effects=True, vmem_limit_bytes=60 * 1024 * 1024
            ),
        )(source_positions, detector_positions, absorption, residual_codes, warm_sources, warm_detectors, labels)
        return pl.pallas_call(
            hand_over,
            out_shape=tuple(jax.ShapeDtypeStruct(r.shape, r.dtype) for r in results),
            in_specs=[hbm] * 3,
            out_specs=(hbm,) * 3,
            scratch_shapes=[*(pltpu.VMEM(r.shape, r.dtype) for r in results), sem((2, 3))],
        )(*results)

    fields = P(("recon", "grp"), "space", None, None)
    return jax.shard_map(
        local,
        mesh=mesh,
        in_specs=(
            fields,
            fields,
            P(("recon", "grp")),
            P(("recon", "grp")),
            P(("recon", "space"), None, None),
            P(),
            P("recon", None),
        ),
        out_specs=(fields, fields, P(("recon", "space"), "grp", None)),
        check_vma=False,
    )
```
